256 devices in a mesh: tile: 2 (over core), pts: 16 (over y, x), grp: 8 (over z).
Axes of the slice: x: 4, y: 4, z: 8, core: 2. Of those that a mesh axis runs over, the one named last changes fastest.
Arguments:
- lidar_features: bfloat16 [262144, 128], P(('tile', 'pts', 'grp')), parts along dimension 0, may hold values from -6 to 6
- reorder_targets: int32 [1, 262144], P(None, ('tile', 'pts', 'grp')), parts along dimension 1, may hold values from 0 to 131071, as said below
- adjacency_targets: int32 [1, 27, 262144], P(None, None, ('tile', 'pts', 'grp')), parts along dimension 2, may hold values from -1 to 131071, as said below
- spatial_stencil_coefficients: bfloat16 [1, 27, 128, 128], replicated, may hold values from -0.15625 to 0.15625
- triple_lens_coefficients: bfloat16 [1, 128, 384], replicated, may hold values from -0.5 to 0.5
- logit_sharpness: float32 [1, 8], replicated, may hold values from 2 to 12
- mixer_exit_coefficients: bfloat16 [1, 128, 128], replicated, may hold values from -0.5 to 0.5
- film_coefficients: float32 [512], P('tile'), parts along dimension 0, may hold values from -3 to 3
- widening_coefficients: bfloat16 [1, 128, 512], replicated, may hold values from -0.5 to 0.5
- narrowing_coefficients: bfloat16 [1, 512, 128], replicated, may hold values from -0.25 to 0.25
Outputs:
- features: bfloat16 [262144, 128], P(('tile', 'pts', 'grp')), parts along dimension 0
The draws below stay inside these ranges and needn't reach their ends.
There are 2 independent parts, one for each index of `tile`. The reference program is written for one: setup_inputs(seed, part) draws one part's arguments, and reference() takes and returns one part's arrays. A program takes and returns all parts, laid end to end along the dimension named above; an argument that names none is the same for every part. Nothing has to cross between parts.
Inputs may be any that keep to these rules, and one draw needn't show every extreme that they name: `reorder_targets`: each block's row is a permutation of 0 to 131071. The 1024 rows of one device send at most 16 points to any one device's rows, and exactly 16 to some device. `adjacency_targets`: entry t = 13 is the point itself; every other present neighbour lies within 128 positions of the point in the new order.
All inputs are finite; a program needn't handle non-finite values.
Results may differ from the reference program's by a relative error of at most 0.0065.
Values may be sent and summed in bfloat16 or wider, within the bound.
A program may use at most 64 MiB of HBM per device.

```python
import math
import jax
import jax.numpy as jnp
from jax import lax

C = 128
HID = 512
FOCUS_TOTAL = 8
KERNEL = 27
PATCH = 1024
HALO = 128
LAYER_TOTAL = 1
PTS_DEV = 1024
POINTS = 131072


def draw_reorder_targets(key, part):
    key = jax.random.fold_in(key, 11)
    device_count = POINTS // PTS_DEV
    share = PTS_DEV // device_count
    block_keys = jax.random.split(key, LAYER_TOTAL)
    results = []
    for layer_ordinal in range(LAYER_TOTAL):
        first_key, second_key, third_key = jax.random.split(block_keys[layer_ordinal], 3)
        first_perm = jax.random.permutation(first_key, device_count).astype(jnp.int32)
        second_perm = jnp.roll(first_perm, -1)
        local_rows = jnp.arange(PTS_DEV, dtype=jnp.int32)
        base_dest = local_rows % device_count
        rank_ids = local_rows // device_count
        shifted = base_dest[None, :] == second_perm[:, None]
        destination = jnp.where(shifted, first_perm[:, None], base_dest[None, :])
        rank_full = rank_ids[None, :] + jnp.where(shifted, share, 0)
        columns = jnp.arange(device_count, dtype=jnp.int32)[None, :]
        loads = share + share * (columns == first_perm[:, None]).astype(jnp.int32) - share * (columns == second_perm[:, None]).astype(jnp.int32)
        offsets = jnp.cumsum(loads, axis=0) - loads
        position = jnp.take_along_axis(offsets, destination, axis=1) + rank_full
        base_table = jnp.tile(jnp.arange(PTS_DEV, dtype=jnp.int32)[None, :], (device_count, 1))
        shuffle = jax.random.permutation(second_key, base_table, axis=1, independent=True)
        positions = destination * PTS_DEV + shuffle[destination, position]
        positions = jax.random.permutation(third_key, positions, axis=1, independent=True)
        results.append(positions.reshape(-1).astype(jnp.int32))
    return jnp.stack(results, axis=0)


def draw_adjacency_targets(key, part):
    key = jax.random.fold_in(key, 23)
    offset_key, present_key = jax.random.split(key)
    offsets = jax.random.randint(offset_key, (LAYER_TOTAL, KERNEL, POINTS), -HALO, HALO + 1, dtype=jnp.int32)
    present = jax.random.randint(present_key, (LAYER_TOTAL, KERNEL, POINTS), 0, 2, dtype=jnp.int32) == 1
    centre = (jnp.arange(KERNEL, dtype=jnp.int32) == KERNEL // 2)[None, :, None]
    offsets = jnp.where(centre, 0, offsets)
    present = present | centre
    targets = jnp.arange(POINTS, dtype=jnp.int32)[None, None, :] + offsets
    inside = present & (targets >= 0) & (targets < POINTS)
    return jnp.where(inside, targets, -1).astype(jnp.int32)


def level_of(stream_key, shape, cuts, low, high):
    level = 1.0
    for dim, blocks in cuts:
        heights = jax.random.uniform(jax.random.fold_in(jax.random.fold_in(stream_key, 6), dim), (blocks,), jnp.float32, low / len(cuts), high / len(cuts))
        level = level * jnp.repeat(jnp.exp(heights), shape[dim] // blocks).reshape((-1,) + (1,) * (len(shape) - 1 - dim))
    return level


def bell_draw(stream_key, dims, width, bound, cuts=(), kind=jnp.bfloat16):
    gain = level_of(stream_key, dims, cuts, -0.22, 0.18) if cuts else 1.0
    values = jax.random.normal(stream_key, dims, jnp.float32) * width * gain
    return jnp.minimum(jnp.maximum(values, -bound), bound).astype(kind)


def setup_inputs(seed: int = 0, part: int = 0) -> dict:
    streams_of = jax.random.split(jax.random.key(seed), 11)
    own_keys = jax.random.split(jax.random.fold_in(streams_of[10], part), 11)
    return {
        "lidar_features": bell_draw(own_keys[0], (POINTS, C), 1.0, 6.0, ((0, 128),)),
        "reorder_targets": draw_reorder_targets(jax.random.fold_in(jax.random.fold_in(streams_of[10], part), 71), part),
        "adjacency_targets": draw_adjacency_targets(jax.random.fold_in(jax.random.fold_in(streams_of[10], part), 71), part),
        "spatial_stencil_coefficients": bell_draw(streams_of[3], (LAYER_TOTAL, KERNEL, C, C), (KERNEL * C // 2) ** -0.5, 0.15625),
        "triple_lens_coefficients": bell_draw(streams_of[4], (LAYER_TOTAL, C, 3 * C), C ** -0.5, 0.5),
        "logit_sharpness": jnp.clip(jnp.exp(jax.random.uniform(streams_of[5], (LAYER_TOTAL, FOCUS_TOTAL), jnp.float32, math.log(2.0), math.log(12.0))), 2.0, 12.0),
        "mixer_exit_coefficients": bell_draw(streams_of[6], (LAYER_TOTAL, C, C), C ** -0.5, 0.5),
        "film_coefficients": bell_draw(own_keys[7], (LAYER_TOTAL * 2 * C,), 0.5, 3.0, (), jnp.float32),
        "widening_coefficients": bell_draw(streams_of[8], (LAYER_TOTAL, C, HID), C ** -0.5, 0.5),
        "narrowing_coefficients": bell_draw(streams_of[9], (LAYER_TOTAL, HID, C), HID ** -0.5, 0.25),
    }


def normalize(values):
    average = lax.optimization_barrier(jnp.mean(values, axis=-1, keepdims=True))
    centred = values - average
    spread = lax.optimization_barrier(jnp.mean(centred * centred, axis=-1, keepdims=True))
    return centred * lax.rsqrt(spread + 1e-05)

def unit_heads(block_vals, focus_total):
    shaped = block_vals.reshape(block_vals.shape[0], focus_total, -1)
    power = lax.optimization_barrier(jnp.mean(shaped * shaped, axis=-1, keepdims=True))
    return (shaped * lax.rsqrt(jnp.maximum(power, 0.25))).astype(jnp.bfloat16)

def patch_group(patch_entries, gathered_entries, stencil_coefficients, triple_lens_local, logit_sharpness_local, mixer_exit_coefficients_local, film_gain_vector, film_bias_vector, widen_coefficients, shrink_coefficients):
    channels = patch_entries.shape[1]
    convolved = lax.dot_general(gathered_entries, stencil_coefficients, (((0, 2), (0, 1)), ((), ())), preferred_element_type=jnp.float32)
    after_conv = patch_entries.astype(jnp.float32) + normalize(convolved)
    normed = normalize(after_conv).astype(jnp.bfloat16)
    projected = jnp.dot(normed, triple_lens_local, preferred_element_type=jnp.float32)
    focus_total = logit_sharpness_local.shape[0]
    focus_breadth = channels // focus_total
    unit_queries = unit_heads(projected[:, :channels], focus_total)
    unit_keys = unit_heads(projected[:, channels:2 * channels], focus_total)
    values = projected[:, 2 * channels:].reshape(-1, focus_total, focus_breadth).astype(jnp.bfloat16)
    head_outputs = []
    for focus_ordinal in range(focus_total):
        affinity_logits = lax.dot_general(unit_queries[:, focus_ordinal], unit_keys[:, focus_ordinal], (((1,), (1,)), ((), ())), preferred_element_type=jnp.float32)
        affinity_logits = affinity_logits * (logit_sharpness_local[focus_ordinal] / focus_breadth)
        expo = jnp.exp(affinity_logits)
        totals = lax.optimization_barrier(jnp.sum(expo, axis=-1, keepdims=True))
        weighted = jnp.dot(expo.astype(jnp.bfloat16), values[:, focus_ordinal], preferred_element_type=jnp.float32)
        head_outputs.append(weighted / totals)
    mixed = jnp.concatenate(head_outputs, axis=-1).astype(jnp.bfloat16)
    after_attn = after_conv + jnp.dot(mixed, mixer_exit_coefficients_local, preferred_element_type=jnp.float32)
    film_input = (normalize(after_attn) * (1.0 + film_gain_vector) + film_bias_vector).astype(jnp.bfloat16)
    hidden = jax.nn.gelu(jnp.dot(film_input, widen_coefficients, preferred_element_type=jnp.float32), approximate=True).astype(jnp.bfloat16)
    after_mlp = after_attn + jnp.dot(hidden, shrink_coefficients, preferred_element_type=jnp.float32)
    return after_mlp.astype(jnp.bfloat16)

def reference(lidar_features, reorder_targets, adjacency_targets, spatial_stencil_coefficients, triple_lens_coefficients, logit_sharpness, mixer_exit_coefficients, film_coefficients, widening_coefficients, narrowing_coefficients):
    point_count, channels = lidar_features.shape
    film_layer_grid = film_coefficients.reshape(LAYER_TOTAL, 2, channels)
    stream = lidar_features
    for layer_ordinal in range(LAYER_TOTAL):
        stream = jnp.zeros_like(stream).at[reorder_targets[layer_ordinal]].set(stream)
        filled_entries = jnp.concatenate([stream, jnp.zeros((1, channels), jnp.bfloat16)], axis=0)
        gather_rows = jnp.where(adjacency_targets[layer_ordinal] < 0, point_count, adjacency_targets[layer_ordinal]).astype(jnp.int32)

        def per_patch(first_row):
            entry_ordinals = lax.dynamic_slice_in_dim(gather_rows, first_row, PATCH, 1)
            patch_entries = lax.dynamic_slice_in_dim(stream, first_row, PATCH, 0)
            return patch_group(patch_entries, filled_entries[entry_ordinals], spatial_stencil_coefficients[layer_ordinal], triple_lens_coefficients[layer_ordinal], logit_sharpness[layer_ordinal], mixer_exit_coefficients[layer_ordinal], film_layer_grid[layer_ordinal, 0], film_layer_grid[layer_ordinal, 1], widening_coefficients[layer_ordinal], narrowing_coefficients[layer_ordinal])
        firsts = jnp.arange(point_count // PATCH, dtype=jnp.int32) * PATCH
        stream = lax.map(per_patch, firsts).reshape(point_count, channels)
    return stream
```

```python
import functools

import jax
import jax.numpy as jnp
from jax import lax
from jax.experimental import pallas as pl
from jax.experimental.pallas import tpu as pltpu
from jax.sharding import PartitionSpec as P

MESH = pl.DeviceIdType.MESH
F32, BF16, I32 = jnp.float32, jnp.bfloat16, jnp.int32
ROWS = 1024
C = 128
HALO = 128
HEADS = 8
TAPS = 27
EXT = ROWS + 2 * HALO
BLK = 256
LOG2E = 1.4426950408889634


def dot(a, b):
    return jnp.dot(a, b, preferred_element_type=F32)


def dot_nt(a, b):
    return lax.dot_general(a, b, (((1,), (1,)), ((), ())), preferred_element_type=F32)


def onehot(mask):
    return jnp.where(mask, 1.0, 0.0).astype(BF16)


def iota(shape, dim):
    return lax.broadcasted_iota(I32, shape, dim)


def z_peer(dz):
    return (lax.axis_index("tile"), lax.axis_index("pts"), (lax.axis_index("grp") + dz) & 7)


def xy_peer(half, idx):
    me = lax.axis_index("pts")
    dy = idx >> 1
    dx = 2 * (idx & 1) + ((half + dy) & 1)
    return (
        lax.axis_index("tile"),
        (((me >> 2) + dy) & 3) * 4 + (((me & 3) + dx) & 3),
        lax.axis_index("grp"),
    )


def slab_peer(step):
    me = (lax.axis_index("pts") * 8 + lax.axis_index("grp") + step) & 127
    return (lax.axis_index("tile"), me >> 3, me & 7)


def reorder_kernel(
    x_ref, target_ref, ext_ref, send, mid, land, msend, mmid, mland, rim, ssem, rsem, hsem
):
    pts, grp = lax.axis_index("pts"), lax.axis_index("grp")
    peers = [z_peer(i) for i in range(1, 8)]
    peers += [xy_peer(0, i) for i in range(1, 8)] + [xy_peer(1, i) for i in range(8)]
    peers += [slab_peer(1), slab_peer(-1)]
    barrier = pltpu.get_barrier_semaphore()
    for peer in peers:
        pl.semaphore_signal(barrier, inc=1, device_id=peer, device_id_type=MESH)

    target = target_ref[...]
    owner = target >> 10
    dy = ((owner >> 5) - (pts >> 2)) & 3
    dx = ((owner >> 3) - (pts & 3)) & 3
    dz = (owner - grp) & 7
    flat = dy * 2 + (dx >> 1)
    group = jnp.where(((dx + dy) & 1) == 0, dz * 8 + flat, 64 + flat * 8 + dz)
    member = iota((128, ROWS), 0) == group
    member_bf = onehot(member)
    earlier = onehot(iota((BLK, BLK), 0) < iota((BLK, BLK), 1))
    carry = jnp.zeros((128, 1), F32)
    ranks = []
    for b in range(ROWS // BLK):
        cols = slice(b * BLK, (b + 1) * BLK)
        part = member_bf[:, cols]
        count = dot(part, earlier) + carry
        ranks.append(jnp.sum(jnp.where(member[:, cols], count, 0.0), axis=0, keepdims=True))
        if b < ROWS // BLK - 1:
            carry = carry + jnp.sum(part.astype(F32), axis=1, keepdims=True)
    rank = jnp.concatenate(ranks, axis=1).astype(I32)
    slot = group * 16 + rank
    lane = ((group >> 3) & 7) * 16 + rank
    place = (target & 1023) + 1
    here = iota((128, ROWS), 0) == lane
    high = jnp.where(here, (place >> 5).astype(F32), 0.0).astype(BF16)
    low = jnp.where(here, (place & 31).astype(F32), 0.0).astype(BF16)
    meta = (32.0 * dot_nt(member_bf, high) + dot_nt(member_bf, low)).reshape(16, 8, 128)
    msend[...] = meta
    mmid[0] = meta[0]

    pl.semaphore_wait(barrier, len(peers))

    def remote(kind, stage, idx, src, dst, peer):
        return pltpu.make_async_remote_copy(
            src, dst, ssem.at[kind, stage, idx], rsem.at[kind, stage, idx],
            device_id=peer, device_id_type=MESH,
        )

    def stage_copies(kind, one, two, three):
        first = [remote(kind, 0, i, one.at[i], two.at[i], z_peer(i)) for i in range(1, 8)]
        second = [remote(kind, 1, i, one.at[8 + i], two.at[8 + i], xy_peer(1, i)) for i in range(8)]
        third = [
            remote(kind, 2, i, two.at[0:8, i], three.at[i], xy_peer(0, i)) for i in range(1, 8)
        ]
        fourth = [
            remote(kind, 3, i, two.at[8:16, i], three.at[8 + i], z_peer(i)) for i in range(1, 8)
        ]
        return first, second, third, fourth

    meta_copies = stage_copies(0, msend, mmid, mland)
    data_copies = stage_copies(1, send, mid, land)

    def start(copies):
        for copy in copies:
            copy.start()

    def arrived(copies):
        for copy in copies:
            copy.wait_recv()

    start(meta_copies[0])
    start(meta_copies[1])
    x = x_ref[...]

    def pack(m0):
        hit = onehot(iota((512, ROWS), 0) + m0 * 128 == slot)
        return dot(hit, x).astype(BF16).reshape(4, 8, 16, C)

    for m0 in (8, 12):
        send[m0 : m0 + 4] = pack(m0)
        start(data_copies[1][m0 - 8 : m0 - 4])
    packed = pack(0)
    send[0:4] = packed
    mid[0] = packed[0]
    start(data_copies[0][0:3])
    send[4:8] = pack(4)
    start(data_copies[0][3:7])

    arrived(meta_copies[0])
    start(meta_copies[2])
    mland[0] = mmid[0:8, 0]
    arrived(meta_copies[1])
    start(meta_copies[3])
    mland[8] = mmid[8:16, 0]
    arrived(data_copies[1])
    start(data_copies[3])
    land[8] = mid[8:16, 0]
    arrived(data_copies[0])
    start(data_copies[2])
    land[0] = mid[0:8, 0]
    arrived(meta_copies[2])
    arrived(meta_copies[3])
    places = jnp.sum(mland[...], axis=1)

    def unpack(m0):
        total = jnp.zeros((ROWS, C), F32)
        for m in range(m0, m0 + 8, 2):
            want = jnp.concatenate([places[m : m + 1], places[m + 1 : m + 2]], axis=1)
            hit = onehot((iota((ROWS, 256), 0) + 1).astype(F32) == want)
            total = total + dot(hit, land[m : m + 2].reshape(256, C))
        return total

    arrived(data_copies[2])
    own = unpack(0)
    arrived(data_copies[3])
    own = (own + unpack(8)).astype(BF16)
    ext_ref[HALO : HALO + ROWS] = own
    rim[0] = own[:HALO]
    rim[1] = own[ROWS - HALO :]
    down = pltpu.make_async_remote_copy(
        rim.at[0], rim.at[2], hsem.at[0], hsem.at[1], device_id=slab_peer(-1), device_id_type=MESH
    )
    up = pltpu.make_async_remote_copy(
        rim.at[1], rim.at[3], hsem.at[2], hsem.at[3], device_id=slab_peer(1), device_id_type=MESH
    )
    down.start()
    up.start()
    for copies in meta_copies + data_copies:
        for copy in copies:
            copy.wait_send()
    up.wait()
    ext_ref[0:HALO] = rim[3]
    down.wait()
    ext_ref[HALO + ROWS :] = rim[2]


def reorder(x, target):
    vmem = pl.BlockSpec(memory_space=pltpu.VMEM)
    return pl.pallas_call(
        reorder_kernel,
        out_shape=jax.ShapeDtypeStruct((EXT, C), BF16),
        in_specs=[vmem, vmem],
        out_specs=vmem,
        scratch_shapes=[pltpu.VMEM((16, 8, 16, C), BF16)] * 3
        + [pltpu.VMEM((16, 8, 128), F32)] * 3
        + [
            pltpu.VMEM((4, HALO, C), BF16),
            pltpu.SemaphoreType.DMA((2, 4, 8)),
            pltpu.SemaphoreType.DMA((2, 4, 8)),
            pltpu.SemaphoreType.DMA((4,)),
        ],
        compiler_params=pltpu.CompilerParams(
            collective_id=0, has_side_effects=True, vmem_limit_bytes=48 << 20
        ),
    )(x, target)


def normalize(values):
    average = jnp.mean(values, axis=-1, keepdims=True)
    centred = values - average
    spread = jnp.mean(centred * centred, axis=-1, keepdims=True)
    return centred * lax.rsqrt(spread + 1e-05)


def head_power(values, spread):
    squares = values * values
    top = squares.astype(BF16)
    rest = (squares - top.astype(F32)).astype(BF16)
    return dot(jnp.concatenate([top, rest], axis=1), spread)


def block_kernel(
    ext_ref, adj_ref, stencil_ref, lens_ref, sharp_ref, mixer_ref, film_ref, wide_ref, narrow_ref,
    out_ref, hits, sides, gathered, conv, queries, keys, vals, mixed,
):
    first = (lax.axis_index("pts") * 8 + lax.axis_index("grp")) * ROWS
    lanes = iota((BLK, BLK), 1)
    for b in range(ROWS // BLK):
        rows = slice(b * BLK, (b + 1) * BLK)
        adj = adj_ref[:, rows]
        rel = jnp.where(adj < 0, -1, adj - (first + b * BLK - HALO))
        rel = jnp.concatenate([rel, jnp.full((32 - TAPS, BLK), -1, I32)], axis=0)
        rel = jnp.transpose(rel.astype(F32), (1, 0)).astype(I32)
        for t in range(TAPS):
            col = rel[:, t : t + 1]
            near = jnp.where(col < 0, -1, col & 255)
            hits[t, rows] = onehot(lanes == near)
            sides[t, rows] = onehot(jnp.broadcast_to(col >= 256, (BLK, C)))
    for b in range(ROWS // BLK):
        rows = slice(b * BLK, (b + 1) * BLK)
        pair = jnp.concatenate(
            [ext_ref[b * BLK : (b + 1) * BLK], ext_ref[(b + 1) * BLK : (b + 2) * BLK]], axis=1
        )
        for t in range(TAPS):
            both = dot(hits[t, rows], pair).astype(BF16)
            gathered[rows, t * C : (t + 1) * C] = jnp.where(
                sides[t, rows] > 0.5, both[:, C:], both[:, :C]
            )
        conv[rows] = dot(gathered[rows], stencil_ref[...])
    after_conv = ext_ref[HALO : HALO + ROWS].astype(F32) + normalize(conv[...])
    conv[...] = after_conv
    normed = normalize(after_conv).astype(BF16)
    projected = dot(normed, lens_ref[...])
    same = (iota((2 * C, C), 0) & 127) >> 4 == iota((2 * C, C), 1) >> 4
    spread = jnp.where(same, 1.0 / 16, 0.0).astype(BF16)
    q, k = projected[:, :C], projected[:, C : 2 * C]
    queries[...] = (q * lax.rsqrt(jnp.maximum(head_power(q, spread), 0.25))).astype(BF16)
    unit_keys = k * lax.rsqrt(jnp.maximum(head_power(k, spread), 0.25))
    keys[...] = jnp.transpose(unit_keys, (1, 0)).astype(BF16)
    values = projected[:, 2 * C :].astype(BF16)
    head_of = iota((ROWS, C), 1) >> 4
    for h in range(HEADS):
        vals[h] = jnp.concatenate(
            [jnp.where(head_of == h, values, jnp.zeros_like(values)), onehot(head_of == h)], axis=1
        )

    def attend(b, carry):
        rows = pl.ds(pl.multiple_of(b * BLK, BLK), BLK)
        q_blk = queries[rows]
        head = iota((BLK, C), 1) >> 4
        total = jnp.zeros((BLK, 2 * C), F32)
        for h in range(HEADS):
            q_head = jnp.where(head == h, q_blk, jnp.zeros_like(q_blk))
            scores = dot(q_head, keys[...]) * (sharp_ref[0, h] * (LOG2E / 16))
            total = total + dot(jnp.exp2(scores).astype(BF16), vals[h])
        mixed[rows] = (total[:, :C] / total[:, C:]).astype(BF16)
        return carry

    lax.fori_loop(0, ROWS // BLK, attend, 0)
    after_attn = conv[...] + dot(mixed[...], mixer_ref[...])
    film_input = (normalize(after_attn) * (1.0 + film_ref[0:1]) + film_ref[1:2]).astype(BF16)
    hidden = jax.nn.gelu(dot(film_input, wide_ref[...]), approximate=True).astype(BF16)
    out_ref[...] = (after_attn + dot(hidden, narrow_ref[...])).astype(BF16)


def block(ext, adjacency, stencil, lens, sharp, mixer, film, wide, narrow):
    vmem = pl.BlockSpec(memory_space=pltpu.VMEM)
    smem = pl.BlockSpec(memory_space=pltpu.SMEM)
    return pl.pallas_call(
        block_kernel,
        out_shape=jax.ShapeDtypeStruct((ROWS, C), BF16),
        in_specs=[vmem] * 4 + [smem] + [vmem] * 4,
        out_specs=vmem,
        scratch_shapes=[
            pltpu.VMEM((TAPS, ROWS, BLK), BF16),
            pltpu.VMEM((TAPS, ROWS, C), BF16),
            pltpu.VMEM((ROWS, TAPS * C), BF16),
            pltpu.VMEM((ROWS, C), F32),
            pltpu.VMEM((ROWS, C), BF16),
            pltpu.VMEM((C, ROWS), BF16),
            pltpu.VMEM((HEADS, ROWS, 2 * C), BF16),
            pltpu.VMEM((ROWS, C), BF16),
        ],
        compiler_params=pltpu.CompilerParams(vmem_limit_bytes=56 << 20),
    )(ext, adjacency, stencil, lens, sharp, mixer, film, wide, narrow)


def shards(features, targets, adjacency, stencil, lens, sharp, mixer, film, wide, narrow):
    ext = reorder(features, targets)
    return block(
        ext, adjacency[0], stencil[0].reshape(TAPS * C, C), lens[0], sharp, mixer[0],
        film.reshape(2, C), wide[0], narrow[0],
    )


def solution(mesh):
    rows = P(("tile", "pts", "grp"), None)
    in_specs = (
        rows,
        P(None, ("tile", "pts", "grp")),
        P(None, None, ("tile", "pts", "grp")),
        P(), P(), P(), P(), P("tile"), P(), P(),
    )
    return jax.shard_map(shards, mesh=mesh, in_specs=in_specs, out_specs=rows, check_vma=False)
```

```python
import functools

import jax
import jax.numpy as jnp
from jax import lax
from jax.experimental import pallas as pl
from jax.experimental.pallas import tpu as pltpu
from jax.sharding import PartitionSpec as P

MESH = pl.DeviceIdType.MESH
F32, BF16, I32 = jnp.float32, jnp.bfloat16, jnp.int32
ROWS = 1024
C = 128
HALO = 128
HEADS = 8
TAPS = 27
EXT = ROWS + 2 * HALO
BLK = 256
LOG2E = 1.4426950408889634


def dot(a, b):
    return jnp.dot(a, b, preferred_element_type=F32)


def dot_nt(a, b):
    return lax.dot_general(a, b, (((1,), (1,)), ((), ())), preferred_element_type=F32)


def onehot(mask):
    return jnp.where(mask, 1.0, 0.0).astype(BF16)


def flip(values):
    return jnp.transpose(values.astype(F32), (1, 0))


def iota(shape, dim):
    return lax.broadcasted_iota(I32, shape, dim)


def z_peer(dz):
    return (lax.axis_index("tile"), lax.axis_index("pts"), (lax.axis_index("grp") + dz) & 7)


def xy_peer(half, idx):
    me = lax.axis_index("pts")
    dy = idx >> 1
    dx = 2 * (idx & 1) + ((half + dy) & 1)
    return (
        lax.axis_index("tile"),
        (((me >> 2) + dy) & 3) * 4 + (((me & 3) + dx) & 3),
        lax.axis_index("grp"),
    )


def slab_peer(step):
    me = (lax.axis_index("pts") * 8 + lax.axis_index("grp") + step) & 127
    return (lax.axis_index("tile"), me >> 3, me & 7)


def block_kernel(
    x_hbm, target_hbm, adj_hbm, stencil_hbm, lens_hbm, sharp_ref, mixer_hbm, film_ref, wide_hbm,
    narrow_hbm, out_ref, x, target_in, adj_in, stencil_in, lens_in, mixer_in, wide_in, narrow_in,
    send, mid, land, msend, mmid, mland, rim, wants, hits, sides, ext, gathered, conv,
    stencil, lens, mixer, wide, narrow, keys, ssem, rsem, hsem, isem,
):
    pts, grp = lax.axis_index("pts"), lax.axis_index("grp")
    loads = [
        pltpu.make_async_copy(src, dst, isem.at[i])
        for i, (src, dst) in enumerate(
            (
                (target_hbm, target_in), (x_hbm, x), (adj_hbm, adj_in), (lens_hbm, lens_in),
                (mixer_hbm, mixer_in), (wide_hbm, wide_in), (narrow_hbm, narrow_in),
                (stencil_hbm, stencil_in),
            )
        )
    ]
    loads[0].start()
    loads[1].start()
    peers = [z_peer(i) for i in range(1, 8)]
    peers += [xy_peer(0, i) for i in range(1, 8)] + [xy_peer(1, i) for i in range(8)]
    peers += [slab_peer(1), slab_peer(-1)]
    barrier = pltpu.get_barrier_semaphore()
    for peer in peers:
        pl.semaphore_signal(barrier, inc=1, device_id=peer, device_id_type=MESH)
    for load in loads[2:]:
        load.start()

    loads[0].wait()
    target = target_in[...]
    owner = target >> 10
    dy = ((owner >> 5) - (pts >> 2)) & 3
    dx = ((owner >> 3) - (pts & 3)) & 3
    dz = (owner - grp) & 7
    flat = dy * 2 + (dx >> 1)
    group = jnp.where(((dx + dy) & 1) == 0, dz * 8 + flat, 64 + flat * 8 + dz)
    member = iota((128, ROWS), 0) == group
    member_bf = onehot(member)
    earlier = onehot(iota((BLK, BLK), 0) < iota((BLK, BLK), 1))
    carry = jnp.zeros((128, 1), F32)
    ranks = []
    for b in range(ROWS // BLK):
        cols = slice(b * BLK, (b + 1) * BLK)
        part = member_bf[:, cols]
        count = dot(part, earlier) + carry
        ranks.append(jnp.sum(jnp.where(member[:, cols], count, 0.0), axis=0, keepdims=True))
        if b < ROWS // BLK - 1:
            carry = carry + jnp.sum(part.astype(F32), axis=1, keepdims=True)
    rank = jnp.concatenate(ranks, axis=1).astype(I32)
    slot = group * 16 + rank
    lane = ((group >> 3) & 7) * 16 + rank
    place = (target & 1023) + 1
    here = iota((128, ROWS), 0) == lane
    high = jnp.where(here, (place >> 5).astype(F32), 0.0).astype(BF16)
    low = jnp.where(here, (place & 31).astype(F32), 0.0).astype(BF16)
    meta = (32.0 * dot_nt(member_bf, high) + dot_nt(member_bf, low)).reshape(16, 8, 128)
    msend[...] = meta
    mmid[0] = meta[0]
    loads[1].wait()

    def pack(m0):
        hit = onehot(iota((512, ROWS), 0) + m0 * 128 == slot)
        return dot(hit, x[...]).astype(BF16).reshape(4, 8, 16, C)

    packed = pack(0)
    send[0:4] = packed
    mid[0] = packed[0]

    pl.semaphore_wait(barrier, len(peers))

    def remote(kind, stage, idx, src, dst, peer):
        return pltpu.make_async_remote_copy(
            src, dst, ssem.at[kind, stage, idx], rsem.at[kind, stage, idx],
            device_id=peer, device_id_type=MESH,
        )

    def stage_copies(kind, one, two, three):
        first = [remote(kind, 0, i, one.at[i], two.at[i], z_peer(i)) for i in range(1, 8)]
        second = [remote(kind, 1, i, one.at[8 + i], two.at[8 + i], xy_peer(1, i)) for i in range(8)]
        third = [
            remote(kind, 2, i, two.at[0:8, i], three.at[i], xy_peer(0, i)) for i in range(1, 8)
        ]
        fourth = [
            remote(kind, 3, i, two.at[8:16, i], three.at[8 + i], z_peer(i)) for i in range(1, 8)
        ]
        return first, second, third, fourth

    meta_copies = stage_copies(0, msend, mmid, mland)
    data_copies = stage_copies(1, send, mid, land)

    def start(copies):
        for copy in copies:
            copy.start()

    def arrived(copies):
        for copy in copies:
            copy.wait_recv()

    start(data_copies[0][0:3])
    send[4:8] = pack(4)
    start(data_copies[0][3:7])
    for m0 in (8, 12):
        send[m0 : m0 + 4] = pack(m0)
        start(data_copies[1][m0 - 8 : m0 - 4])
    start(meta_copies[0])
    start(meta_copies[1])

    first_row = (pts * 8 + grp) * ROWS
    base = first_row - HALO + (iota((1, ROWS), 1) >> 8) * BLK

    def tap_hits(t, carry):
        adj = adj_in[t]
        rel = adj - base
        near = jnp.where(adj < 0, -1, rel & (BLK - 1))
        sides[t] = rel
        hits[t] = onehot(iota((BLK, ROWS), 0) == near)
        return carry

    loads[2].wait()
    lax.fori_loop(0, 9, tap_hits, 0)
    for load in loads[3:]:
        load.wait()
    for i in range(3):
        lens[i * C : (i + 1) * C] = flip(lens_in[:, i * C : (i + 1) * C]).astype(BF16)
    mixer[...] = flip(mixer_in[...]).astype(BF16)
    for i in range(4):
        wide[i * C : (i + 1) * C] = flip(wide_in[:, i * C : (i + 1) * C]).astype(BF16)
        narrow[:, i * C : (i + 1) * C] = flip(narrow_in[i * C : (i + 1) * C]).astype(BF16)
    for t in range(TAPS):
        stencil[:, t * C : (t + 1) * C] = flip(stencil_in[t * C : (t + 1) * C]).astype(BF16)
    film = flip(jnp.concatenate([film_ref[...], jnp.zeros((6, C), F32)], axis=0))

    arrived(data_copies[1])
    start(data_copies[3])
    arrived(meta_copies[0])
    start(meta_copies[2])
    arrived(meta_copies[1])
    start(meta_copies[3])
    mland[0] = mmid[0:8, 0]
    mland[8] = mmid[8:16, 0]
    land[8] = mid[8:16, 0]
    lax.fori_loop(9, 15, tap_hits, 0)
    arrived(data_copies[0])
    start(data_copies[2])
    land[0] = mid[0:8, 0]
    lax.fori_loop(15, TAPS, tap_hits, 0)
    arrived(meta_copies[2])
    arrived(meta_copies[3])
    places = jnp.sum(mland[...], axis=1)
    for m in range(16):
        wants[:, m * C : (m + 1) * C] = onehot(
            (iota((ROWS, C), 0) + 1).astype(F32) == places[m : m + 1]
        )
    half = ROWS
    arrived(data_copies[2])
    own = dot(wants[:, :half], land[0:8].reshape(half, C))
    arrived(data_copies[3])
    own = own + dot(wants[:, half:], land[8:16].reshape(half, C))
    rim[0] = own[:HALO].astype(BF16)
    rim[1] = own[ROWS - HALO :].astype(BF16)
    down = pltpu.make_async_remote_copy(
        rim.at[0], rim.at[2], hsem.at[0], hsem.at[1], device_id=slab_peer(-1), device_id_type=MESH
    )
    up = pltpu.make_async_remote_copy(
        rim.at[1], rim.at[3], hsem.at[2], hsem.at[3], device_id=slab_peer(1), device_id_type=MESH
    )
    down.start()
    up.start()
    ext[:, HALO : HALO + ROWS] = flip(own).astype(BF16)

    def convolve(b):
        at = pl.multiple_of(b * BLK, BLK)
        cols = pl.ds(at, BLK)
        pair = jnp.concatenate(
            [ext[:, cols], ext[:, pl.ds(pl.multiple_of(at + BLK, BLK), BLK)]], axis=0
        )
        for t in range(TAPS):
            both = dot(pair, hits[t, :, cols])
            gathered[t * C : (t + 1) * C] = jnp.where(
                sides[t, :, cols] >= BLK, both[C:], both[:C]
            ).astype(BF16)
        conv[:, cols] = dot(stencil[...], gathered[...])

    lax.fori_loop(1, 3, lambda b, c: (convolve(b), c)[1], 0)
    up.wait()
    ext[:, 0:HALO] = flip(rim[3]).astype(BF16)
    down.wait()
    ext[:, HALO + ROWS :] = flip(rim[2]).astype(BF16)
    lax.fori_loop(0, 2, lambda b, c: (convolve(3 * b), c)[1], 0)

    after_conv = ext[:, HALO : HALO + ROWS].astype(F32) + normalize(conv[...])
    conv[...] = after_conv
    normed = normalize(after_conv).astype(BF16)
    projected = dot(lens[...], normed)

    def unit(values):
        shaped = values.reshape(HEADS, C // HEADS, ROWS)
        power = jnp.mean(shaped * shaped, axis=1, keepdims=True)
        return (shaped * lax.rsqrt(jnp.maximum(power, 0.25))).reshape(C, ROWS)

    queries = unit(projected[:C]).astype(BF16)
    keys[...] = flip(unit(projected[C : 2 * C])).astype(BF16)
    values = projected[2 * C :].astype(BF16)
    ones = jnp.ones((C // HEADS, ROWS), BF16)
    head_of = iota((C, ROWS), 0) >> 4
    mixed = []
    for h in range(HEADS):
        query = jnp.where(head_of == h, queries, jnp.zeros_like(queries))
        value = jnp.concatenate([values[16 * h : 16 * h + 16], ones], axis=0)
        outs = []
        for b in range(2):
            scores = dot(keys[...], query[:, b * 512 : (b + 1) * 512])
            weights = jnp.exp2(scores * (sharp_ref[0, h] * (LOG2E / 16))).astype(BF16)
            sums = dot(value, weights)
            outs.append(sums[:16] / sums[16:])
        mixed.append(jnp.concatenate(outs, axis=1))
    mixed = jnp.concatenate(mixed, axis=0).astype(BF16)
    after_attn = conv[...] + dot(mixer[...], mixed)
    film_input = (normalize(after_attn) * (1.0 + film[:, 0:1]) + film[:, 1:2]).astype(BF16)
    hidden = jax.nn.gelu(dot(wide[...], film_input), approximate=True).astype(BF16)
    out_ref[...] = flip(after_attn + dot(narrow[...], hidden)).astype(BF16)
    for copies in meta_copies + data_copies:
        for copy in copies:
            copy.wait_send()


def normalize(values):
    average = jnp.mean(values, axis=0, keepdims=True)
    centred = values - average
    spread = jnp.mean(centred * centred, axis=0, keepdims=True)
    return centred * lax.rsqrt(spread + 1e-05)


def shards(features, targets, adjacency, stencil, lens, sharp, mixer, film, wide, narrow):
    hbm = pl.BlockSpec(memory_space=pl.ANY)
    vmem = pl.BlockSpec(memory_space=pltpu.VMEM)
    smem = pl.BlockSpec(memory_space=pltpu.SMEM)
    hid = wide.shape[-1]
    return pl.pallas_call(
        block_kernel,
        out_shape=jax.ShapeDtypeStruct((ROWS, C), BF16),
        in_specs=[hbm] * 5 + [smem, hbm, vmem, hbm, hbm],
        out_specs=vmem,
        scratch_shapes=[
            pltpu.VMEM((ROWS, C), BF16),
            pltpu.VMEM((1, ROWS), I32),
            pltpu.VMEM((TAPS, 1, ROWS), I32),
            pltpu.VMEM((TAPS * C, C), BF16),
            pltpu.VMEM((C, 3 * C), BF16),
            pltpu.VMEM((C, C), BF16),
            pltpu.VMEM((C, hid), BF16),
            pltpu.VMEM((hid, C), BF16),
        ]
        + [pltpu.VMEM((16, 8, 16, C), BF16)] * 3
        + [pltpu.VMEM((16, 8, 128), F32)] * 3
        + [
            pltpu.VMEM((4, HALO, C), BF16),
            pltpu.VMEM((ROWS, 2 * ROWS), BF16),
            pltpu.VMEM((TAPS, BLK, ROWS), BF16),
            pltpu.VMEM((TAPS, 1, ROWS), I32),
            pltpu.VMEM((C, EXT), BF16),
            pltpu.VMEM((TAPS * C, BLK), BF16),
            pltpu.VMEM((C, ROWS), F32),
            pltpu.VMEM((C, TAPS * C), BF16),
            pltpu.VMEM((3 * C, C), BF16),
            pltpu.VMEM((C, C), BF16),
            pltpu.VMEM((hid, C), BF16),
            pltpu.VMEM((C, hid), BF16),
            pltpu.VMEM((ROWS, C), BF16),
            pltpu.SemaphoreType.DMA((2, 4, 8)),
            pltpu.SemaphoreType.DMA((2, 4, 8)),
            pltpu.SemaphoreType.DMA((4,)),
            pltpu.SemaphoreType.DMA((8,)),
        ],
        compiler_params=pltpu.CompilerParams(
            collective_id=0, has_side_effects=True, vmem_limit_bytes=56 << 20
        ),
    )(
        features, targets, adjacency.reshape(TAPS, 1, ROWS), stencil.reshape(TAPS * C, C),
        lens[0], sharp, mixer[0], film.reshape(2, C), wide[0], narrow[0],
    )


def solution(mesh):
    rows = P(("tile", "pts", "grp"), None)
    in_specs = (
        rows,
        P(None, ("tile", "pts", "grp")),
        P(None, None, ("tile", "pts", "grp")),
        P(), P(), P(), P(), P("tile"), P(), P(),
    )
    return jax.shard_map(shards, mesh=mesh, in_specs=in_specs, out_specs=rows, check_vma=False)
```

```python
import functools

import jax
import jax.numpy as jnp
from jax import lax
from jax.experimental import pallas as pl
from jax.experimental.pallas import tpu as pltpu
from jax.sharding import PartitionSpec as P

MESH = pl.DeviceIdType.MESH
F32, BF16, I32 = jnp.float32, jnp.bfloat16, jnp.int32
ROWS = 1024
C = 128
HALO = 128
HEADS = 8
TAPS = 27
EXT = ROWS + 2 * HALO
BLK = 256
LOG2E = 1.4426950408889634


def dot(a, b):
    return jnp.dot(a, b, preferred_element_type=F32)


def dot_nt(a, b):
    return lax.dot_general(a, b, (((1,), (1,)), ((), ())), preferred_element_type=F32)


def onehot(mask):
    return jnp.where(mask, 1.0, 0.0).astype(BF16)


def flip(values):
    return jnp.transpose(values.astype(F32), (1, 0))


def iota(shape, dim):
    return lax.broadcasted_iota(I32, shape, dim)


def z_peer(dz):
    return (lax.axis_index("tile"), lax.axis_index("pts"), (lax.axis_index("grp") + dz) & 7)


def xy_peer(half, idx):
    me = lax.axis_index("pts")
    dy = idx >> 1
    dx = 2 * (idx & 1) + ((half + dy) & 1)
    return (
        lax.axis_index("tile"),
        (((me >> 2) + dy) & 3) * 4 + (((me & 3) + dx) & 3),
        lax.axis_index("grp"),
    )


def slab_peer(step):
    me = (lax.axis_index("pts") * 8 + lax.axis_index("grp") + step) & 127
    return (lax.axis_index("tile"), me >> 3, me & 7)


def block_kernel(
    x_hbm, target_hbm, adj_hbm, stencil_hbm, lens_hbm, sharp_ref, mixer_hbm, film_ref, wide_hbm,
    narrow_hbm, out_ref, x, target_in, adj_in, stencil_in, lens_in, mixer_in, wide_in, narrow_in,
    send, mid, land, msend, mmid, mland, wants, hits, sides, ext, gathered, conv,
    stencil, lens, mixer, wide, narrow, keys, ssem, rsem, hsem, isem,
):
    pts, grp = lax.axis_index("pts"), lax.axis_index("grp")
    loads = [
        pltpu.make_async_copy(src, dst, isem.at[i])
        for i, (src, dst) in enumerate(
            (
                (target_hbm, target_in), (x_hbm, x), (adj_hbm, adj_in), (lens_hbm, lens_in),
                (mixer_hbm, mixer_in), (wide_hbm, wide_in), (narrow_hbm, narrow_in),
                (stencil_hbm, stencil_in),
            )
        )
    ]
    loads[0].start()
    loads[1].start()
    peers = [z_peer(i) for i in range(1, 8)]
    peers += [xy_peer(0, i) for i in range(1, 8)] + [xy_peer(1, i) for i in range(8)]
    slab = pts * 8 + grp
    barrier = pltpu.get_barrier_semaphore()

    def greet(peer):
        pl.semaphore_signal(barrier, inc=1, device_id=peer, device_id_type=MESH)

    for peer in peers:
        greet(peer)
    pl.when(slab > 0)(lambda: greet(slab_peer(-1)))
    pl.when(slab < 127)(lambda: greet(slab_peer(1)))
    for load in loads[2:]:
        load.start()

    loads[0].wait()
    target = target_in[...]
    owner = target >> 10
    dy = ((owner >> 5) - (pts >> 2)) & 3
    dx = ((owner >> 3) - (pts & 3)) & 3
    dz = (owner - grp) & 7
    flat = dy * 2 + (dx >> 1)
    odd = (dx + dy) & 1
    group = jnp.where(odd == 0, dz * 8 + flat, 64 + flat * 8 + dz)
    member = iota((128, ROWS), 0) == group
    member_bf = onehot(member)
    earlier = onehot(iota((BLK, BLK), 0) < iota((BLK, BLK), 1))
    carry = jnp.zeros((128, 1), F32)
    ranks = []
    for b in range(ROWS // BLK):
        cols = slice(b * BLK, (b + 1) * BLK)
        part = member_bf[:, cols]
        count = dot(part, earlier) + carry
        ranks.append(jnp.sum(jnp.where(member[:, cols], count, 0.0), axis=0, keepdims=True))
        if b < ROWS // BLK - 1:
            carry = carry + jnp.sum(part.astype(F32), axis=1, keepdims=True)
    rank = jnp.concatenate(ranks, axis=1).astype(I32)
    slot = group * 16 + rank
    lane = ((group >> 3) & 7) * 16 + rank
    place = (target & 1023) + 1
    here = iota((128, ROWS), 0) == lane
    high = jnp.where(here, (place >> 5).astype(F32), 0.0).astype(BF16)
    low = jnp.where(here, (place & 31).astype(F32), 0.0).astype(BF16)
    by_z = onehot(iota((128, ROWS), 0) == dz * 16 + odd * 8 + flat)
    meta = (32.0 * dot_nt(by_z, high) + dot_nt(by_z, low)).reshape(8, 16, 128)
    msend[...] = meta
    mmid[0] = meta[0]
    loads[1].wait()

    def pack(m0):
        hit = onehot(iota((512, ROWS), 0) + m0 * 128 == slot)
        return dot(hit, x[...]).astype(BF16).reshape(4, 8, 16, C)

    packed = pack(0)
    send[0:4] = packed
    mid[0] = packed[0]

    inward = jnp.minimum(slab, 1) + jnp.minimum(127 - slab, 1)
    pl.semaphore_wait(barrier, len(peers) + inward)

    def remote(stage, src, dst, peer):
        return pltpu.make_async_remote_copy(
            src, dst, ssem.at[stage], rsem.at[stage], device_id=peer, device_id_type=MESH
        )

    data_copies = (
        [remote(0, send.at[i], mid.at[i], z_peer(i)) for i in range(1, 8)],
        [remote(1, send.at[8 + i], mid.at[8 + i], xy_peer(1, i)) for i in range(8)],
        [remote(2, mid.at[0:8, i], land.at[i], xy_peer(0, i)) for i in range(1, 8)],
        [remote(3, mid.at[8:16, i], land.at[8 + i], z_peer(i)) for i in range(1, 8)],
    )
    meta_copies = (
        [remote(4, msend.at[i], mmid.at[i], z_peer(i)) for i in range(1, 8)],
        [
            remote(5, mmid.at[0:8, i], mland.at[i], xy_peer(i >> 3, i & 7)) for i in range(1, 16)
        ],
    )
    landed = (
        mid.at[1:8], mid.at[8:16], land.at[1:8], land.at[9:16], mmid.at[1:8], mland.at[1:16]
    )

    def start(copies):
        for copy in copies:
            copy.start()

    def arrived(stage):
        pltpu.make_async_copy(landed[stage], landed[stage], rsem.at[stage]).wait()

    start(data_copies[0][0:3])
    send[4:8] = pack(4)
    start(data_copies[0][3:7])
    for m0 in (8, 12):
        send[m0 : m0 + 4] = pack(m0)
        start(data_copies[1][m0 - 8 : m0 - 4])
    start(meta_copies[0])

    point = iota((1, ROWS), 1)
    inner = (point >= HALO) & (point < ROWS - HALO)
    upper = point >= ROWS - HALO
    base = jnp.where(
        inner, ((point - HALO) >> 8) * BLK, jnp.where(upper, ROWS - 2 * HALO, -HALO)
    )
    base = base + slab * ROWS
    low_bits = jnp.where(inner, BLK - 1, HALO - 1)
    lift = jnp.where(upper, HALO, 0)

    def tap_hits(t, carry):
        adj = adj_in[t]
        rel = adj - base
        near = jnp.where(adj < 0, -1, (rel & low_bits) + lift)
        sides[t] = rel
        hits[t] = onehot(iota((BLK, ROWS), 0) == near)
        return carry

    loads[2].wait()
    lax.fori_loop(0, 9, tap_hits, 0)
    for load in loads[3:]:
        load.wait()
    for i in range(3):
        lens[i * C : (i + 1) * C] = flip(lens_in[:, i * C : (i + 1) * C]).astype(BF16)
    mixer[...] = flip(mixer_in[...]).astype(BF16)
    for i in range(4):
        wide[i * C : (i + 1) * C] = flip(wide_in[:, i * C : (i + 1) * C]).astype(BF16)
        narrow[:, i * C : (i + 1) * C] = flip(narrow_in[i * C : (i + 1) * C]).astype(BF16)
    for t in range(TAPS):
        stencil[:, t * C : (t + 1) * C] = flip(stencil_in[t * C : (t + 1) * C]).astype(BF16)
    film = flip(jnp.concatenate([film_ref[...], jnp.zeros((6, C), F32)], axis=0))

    arrived(1)
    start(data_copies[3])
    arrived(4)
    start(meta_copies[1])
    mland[0] = mmid[0:8, 0]
    land[8] = mid[8:16, 0]
    lax.fori_loop(9, 15, tap_hits, 0)
    arrived(0)
    start(data_copies[2])
    land[0] = mid[0:8, 0]
    lax.fori_loop(15, TAPS, tap_hits, 0)
    arrived(5)
    places = jnp.concatenate([jnp.sum(mland[0:8], axis=1), jnp.sum(mland[8:16], axis=0)], axis=0)
    places = flip(places)
    for m in range(16):
        wants[m * C : (m + 1) * C] = onehot(
            (iota((C, ROWS), 1) + 1).astype(F32) == places[:, m : m + 1]
        )

    def unpack(m0):
        rows = [flip(land[m].reshape(C, C)).astype(BF16) for m in range(m0, m0 + 8)]
        return dot(jnp.concatenate(rows, axis=1), wants[m0 * C : (m0 + 8) * C])

    arrived(2)
    own = unpack(0)
    arrived(3)
    ext[:, HALO : HALO + ROWS] = (own + unpack(8)).astype(BF16)
    down = pltpu.make_async_remote_copy(
        ext.at[:, HALO : 2 * HALO], ext.at[:, EXT - HALO : EXT], hsem.at[0], hsem.at[1],
        device_id=slab_peer(-1), device_id_type=MESH,
    )
    up = pltpu.make_async_remote_copy(
        ext.at[:, ROWS : ROWS + HALO], ext.at[:, 0:HALO], hsem.at[2], hsem.at[3],
        device_id=slab_peer(1), device_id_type=MESH,
    )
    pl.when(slab > 0)(down.start)
    pl.when(slab < 127)(up.start)

    for b in range(3):
        at = HALO + b * BLK
        cols = slice(at, at + BLK)
        pair = jnp.concatenate([ext[:, at : at + BLK], ext[:, at + BLK : at + 2 * BLK]], axis=0)
        for t in range(TAPS):
            both = dot(pair, hits[t, :, cols])
            gathered[t * C : (t + 1) * C, cols] = jnp.where(
                sides[t, :, cols] >= BLK, both[C:], both[:C]
            ).astype(BF16)
        conv[:, cols] = dot(stencil[...], gathered[:, cols])

    @pl.when(slab > 0)
    def _():
        up.wait_recv()

    @pl.when(slab == 0)
    def _():
        ext[:, 0:HALO] = jnp.zeros((C, HALO), BF16)

    @pl.when(slab < 127)
    def _():
        down.wait_recv()

    @pl.when(slab == 127)
    def _():
        ext[:, EXT - HALO : EXT] = jnp.zeros((C, HALO), BF16)

    tail = ROWS - HALO
    trio = jnp.concatenate(
        [
            jnp.concatenate(
                [ext[:, w * HALO : (w + 1) * HALO], ext[:, tail + w * HALO : tail + (w + 1) * HALO]],
                axis=1,
            )
            for w in range(3)
        ],
        axis=0,
    )
    for t in range(TAPS):
        three = dot(trio, jnp.concatenate([hits[t, :, :HALO], hits[t, :, tail:]], axis=1))
        side = jnp.concatenate([sides[t, :, :HALO], sides[t, :, tail:]], axis=1)
        picked = jnp.where(
            side >= HALO, jnp.where(side >= 2 * HALO, three[2 * C :], three[C : 2 * C]), three[:C]
        ).astype(BF16)
        gathered[t * C : (t + 1) * C, :HALO] = picked[:, :HALO]
        gathered[t * C : (t + 1) * C, tail:] = picked[:, HALO:]
    ends = dot(stencil[...], jnp.concatenate([gathered[:, :HALO], gathered[:, tail:]], axis=1))
    conv[:, :HALO] = ends[:, :HALO]
    conv[:, tail:] = ends[:, HALO:]

    after_conv = ext[:, HALO : HALO + ROWS].astype(F32) + normalize(conv[...])
    conv[...] = after_conv
    normed = normalize(after_conv).astype(BF16)
    projected = dot(lens[...], normed)

    def unit(values):
        shaped = values.reshape(HEADS, C // HEADS, ROWS)
        power = jnp.mean(shaped * shaped, axis=1, keepdims=True)
        return (shaped * lax.rsqrt(jnp.maximum(power, 0.25))).reshape(C, ROWS)

    queries = unit(projected[:C]).astype(BF16)
    keys[...] = flip(unit(projected[C : 2 * C])).astype(BF16)
    values = projected[2 * C :].astype(BF16)
    ones = jnp.ones((C // HEADS, ROWS), BF16)
    head_of = iota((C, ROWS), 0) >> 4
    mixed = []
    for h in range(HEADS):
        query = jnp.where(head_of == h, queries, jnp.zeros_like(queries))
        value = jnp.concatenate([values[16 * h : 16 * h + 16], ones], axis=0)
        outs = []
        for b in range(2):
            scores = dot(keys[...], query[:, b * 512 : (b + 1) * 512])
            weights = jnp.exp2(scores * (sharp_ref[0, h] * (LOG2E / 16))).astype(BF16)
            sums = dot(value, weights)
            outs.append(sums[:16] / sums[16:])
        mixed.append(jnp.concatenate(outs, axis=1))
    mixed = jnp.concatenate(mixed, axis=0).astype(BF16)
    after_attn = conv[...] + dot(mixer[...], mixed)
    film_input = (normalize(after_attn) * (1.0 + film[:, 0:1]) + film[:, 1:2]).astype(BF16)
    hidden = jax.nn.gelu(dot(wide[...], film_input), approximate=True).astype(BF16)
    out_ref[...] = flip(after_attn + dot(narrow[...], hidden)).astype(BF16)
    for stage in range(6):
        pltpu.make_async_copy(landed[stage], landed[stage], ssem.at[stage]).wait()
    pl.when(slab > 0)(down.wait_send)
    pl.when(slab < 127)(up.wait_send)


def normalize(values):
    average = jnp.mean(values, axis=0, keepdims=True)
    centred = values - average
    spread = jnp.mean(centred * centred, axis=0, keepdims=True)
    return centred * lax.rsqrt(spread + 1e-05)


def shards(features, targets, adjacency, stencil, lens, sharp, mixer, film, wide, narrow):
    hbm = pl.BlockSpec(memory_space=pl.ANY)
    vmem = pl.BlockSpec(memory_space=pltpu.VMEM)
    smem = pl.BlockSpec(memory_space=pltpu.SMEM)
    hid = wide.shape[-1]
    return pl.pallas_call(
        block_kernel,
        out_shape=jax.ShapeDtypeStruct((ROWS, C), BF16),
        in_specs=[hbm] * 5 + [smem, hbm, vmem, hbm, hbm],
        out_specs=vmem,
        scratch_shapes=[
            pltpu.VMEM((ROWS, C), BF16),
            pltpu.VMEM((1, ROWS), I32),
            pltpu.VMEM((TAPS, 1, ROWS), I32),
            pltpu.VMEM((TAPS * C, C), BF16),
            pltpu.VMEM((C, 3 * C), BF16),
            pltpu.VMEM((C, C), BF16),
            pltpu.VMEM((C, hid), BF16),
            pltpu.VMEM((hid, C), BF16),
        ]
        + [pltpu.VMEM((16, 8, 16, C), BF16)] * 3
        + [pltpu.VMEM((8, 16, 128), F32)] * 2
        + [
            pltpu.VMEM((16, 8, 128), F32),
            pltpu.VMEM((2 * ROWS, ROWS), BF16),
            pltpu.VMEM((TAPS, BLK, ROWS), BF16),
            pltpu.VMEM((TAPS, 1, ROWS), I32),
            pltpu.VMEM((C, EXT), BF16),
            pltpu.VMEM((TAPS * C, ROWS), BF16),
            pltpu.VMEM((C, ROWS), F32),
            pltpu.VMEM((C, TAPS * C), BF16),
            pltpu.VMEM((3 * C, C), BF16),
            pltpu.VMEM((C, C), BF16),
            pltpu.VMEM((hid, C), BF16),
            pltpu.VMEM((C, hid), BF16),
            pltpu.VMEM((ROWS, C), BF16),
            pltpu.SemaphoreType.DMA((6,)),
            pltpu.SemaphoreType.DMA((6,)),
            pltpu.SemaphoreType.DMA((4,)),
            pltpu.SemaphoreType.DMA((8,)),
        ],
        compiler_params=pltpu.CompilerParams(
            collective_id=0, has_side_effects=True, vmem_limit_bytes=56 << 20
        ),
    )(
        features, targets, adjacency.reshape(TAPS, 1, ROWS), stencil.reshape(TAPS * C, C),
        lens[0], sharp, mixer[0], film.reshape(2, C), wide[0], narrow[0],
    )


def solution(mesh):
    rows = P(("tile", "pts", "grp"), None)
    in_specs = (
        rows,
        P(None, ("tile", "pts", "grp")),
        P(None, None, ("tile", "pts", "grp")),
        P(), P(), P(), P(), P("tile"), P(), P(),
    )
    return jax.shard_map(shards, mesh=mesh, in_specs=in_specs, out_specs=rows, check_vma=False)
```

```python
import functools

import jax
import jax.numpy as jnp
from jax import lax
from jax.experimental import pallas as pl
from jax.experimental.pallas import tpu as pltpu
from jax.sharding import PartitionSpec as P

MESH = pl.DeviceIdType.MESH
F32, BF16, I32 = jnp.float32, jnp.bfloat16, jnp.int32
ROWS = 1024
C = 128
HALO = 128
HEADS = 8
TAPS = 27
EXT = ROWS + 2 * HALO
BLK = 256
LOG2E = 1.4426950408889634


def dot(a, b):
    return jnp.dot(a, b, preferred_element_type=F32)


def dot_nt(a, b):
    return lax.dot_general(a, b, (((1,), (1,)), ((), ())), preferred_element_type=F32)


def onehot(mask):
    return jnp.where(mask, 1.0, 0.0).astype(BF16)


def flip(values):
    return jnp.transpose(values.astype(F32), (1, 0))


def iota(shape, dim):
    return lax.broadcasted_iota(I32, shape, dim)


def z_peer(dz):
    return (lax.axis_index("tile"), lax.axis_index("pts"), (lax.axis_index("grp") + dz) & 7)


def xy_peer(half, idx):
    me = lax.axis_index("pts")
    dy = idx >> 1
    dx = 2 * (idx & 1) + ((half + dy) & 1)
    return (
        lax.axis_index("tile"),
        (((me >> 2) + dy) & 3) * 4 + (((me & 3) + dx) & 3),
        lax.axis_index("grp"),
    )


def slab_peer(step):
    me = (lax.axis_index("pts") * 8 + lax.axis_index("grp") + step) & 127
    return (lax.axis_index("tile"), me >> 3, me & 7)


def block_kernel(
    x_hbm, target_hbm, adj_hbm, stencil_hbm, lens_hbm, sharp_ref, mixer_hbm, film_ref, wide_hbm,
    narrow_hbm, out_ref, x, target_in, adj_in, stencil_in, lens_in, mixer_in, wide_in, narrow_in,
    send, mid, land, msend, mmid, mland, wants, hits, sides, ext, gathered, conv,
    stencil, lens, mixer, wide, narrow, keys, ssem, rsem, hsem, isem,
):
    pts, grp = lax.axis_index("pts"), lax.axis_index("grp")
    loads = [
        pltpu.make_async_copy(src, dst, isem.at[i])
        for i, (src, dst) in enumerate(
            (
                (target_hbm, target_in), (x_hbm, x), (adj_hbm, adj_in), (lens_hbm, lens_in),
                (mixer_hbm, mixer_in), (wide_hbm, wide_in), (narrow_hbm, narrow_in),
                (stencil_hbm, stencil_in),
            )
        )
    ]
    loads[0].start()
    loads[1].start()
    peers = [z_peer(i) for i in range(1, 8)]
    peers += [xy_peer(0, i) for i in range(1, 8)] + [xy_peer(1, i) for i in range(8)]
    slab = pts * 8 + grp
    barrier = pltpu.get_barrier_semaphore()

    def greet(peer):
        pl.semaphore_signal(barrier, inc=1, device_id=peer, device_id_type=MESH)

    for peer in peers:
        greet(peer)
    pl.when(slab > 0)(lambda: greet(slab_peer(-1)))
    pl.when(slab < 127)(lambda: greet(slab_peer(1)))
    for load in loads[2:]:
        load.start()

    loads[0].wait()
    target = target_in[...]
    owner = target >> 10
    dy = ((owner >> 5) - (pts >> 2)) & 3
    dx = ((owner >> 3) - (pts & 3)) & 3
    dz = (owner - grp) & 7
    flat = dy * 2 + (dx >> 1)
    odd = (dx + dy) & 1
    group = jnp.where(odd == 0, dz * 8 + flat, 64 + flat * 8 + dz)
    member = iota((128, ROWS), 0) == group
    member_bf = onehot(member)
    earlier = onehot(iota((BLK, BLK), 0) < iota((BLK, BLK), 1))
    carry = jnp.zeros((128, 1), F32)
    ranks = []
    for b in range(ROWS // BLK):
        cols = slice(b * BLK, (b + 1) * BLK)
        part = member_bf[:, cols]
        count = dot(part, earlier) + carry
        ranks.append(jnp.sum(jnp.where(member[:, cols], count, 0.0), axis=0, keepdims=True))
        if b < ROWS // BLK - 1:
            carry = carry + jnp.sum(part.astype(F32), axis=1, keepdims=True)
    rank = jnp.concatenate(ranks, axis=1).astype(I32)
    slot = group * 16 + rank
    loads[1].wait()

    def pack(m0):
        hit = onehot(iota((512, ROWS), 0) + m0 * 128 == slot)
        return dot(hit, x[...]).astype(BF16).reshape(4, 8, 16, C)

    packed = pack(0)
    send[0:4] = packed
    mid[0] = packed[0]

    inward = jnp.minimum(slab, 1) + jnp.minimum(127 - slab, 1)
    pl.semaphore_wait(barrier, len(peers) + inward)

    def remote(stage, src, dst, peer):
        return pltpu.make_async_remote_copy(
            src, dst, ssem.at[stage], rsem.at[stage], device_id=peer, device_id_type=MESH
        )

    data_copies = (
        [remote(0, send.at[i], mid.at[i], z_peer(i)) for i in range(1, 8)],
        [remote(1, send.at[8 + i], mid.at[8 + i], xy_peer(1, i)) for i in range(8)],
        [remote(2, mid.at[0:8, i], land.at[i], xy_peer(0, i)) for i in range(1, 8)],
        [remote(3, mid.at[8:16, i], land.at[8 + i], z_peer(i)) for i in range(1, 8)],
    )
    meta_copies = (
        [remote(4, msend.at[i], mmid.at[i], z_peer(i)) for i in range(1, 8)],
        [
            remote(5, mmid.at[0:8, i], mland.at[i], xy_peer(i >> 3, i & 7)) for i in range(1, 16)
        ],
    )
    landed = (
        mid.at[1:8], mid.at[8:16], land.at[1:8], land.at[9:16], mmid.at[1:8], mland.at[1:16]
    )

    def start(copies):
        for copy in copies:
            copy.start()

    def arrived(stage):
        pltpu.make_async_copy(landed[stage], landed[stage], rsem.at[stage]).wait()

    start(data_copies[0][0:3])
    send[4:8] = pack(4)
    start(data_copies[0][3:7])
    for m0 in (8, 12):
        send[m0 : m0 + 4] = pack(m0)
        start(data_copies[1][m0 - 8 : m0 - 4])
    lane = ((group >> 3) & 7) * 16 + rank
    place = (target & 1023) + 1
    here = iota((128, ROWS), 0) == lane
    high = jnp.where(here, (place >> 5).astype(F32), 0.0).astype(BF16)
    low = jnp.where(here, (place & 31).astype(F32), 0.0).astype(BF16)
    by_z = onehot(iota((128, ROWS), 0) == dz * 16 + odd * 8 + flat)
    meta = (32.0 * dot_nt(by_z, high) + dot_nt(by_z, low)).reshape(8, 16, 128)
    msend[...] = meta
    mmid[0] = meta[0]
    start(meta_copies[0])

    point = iota((1, ROWS), 1)
    inner = (point >= HALO) & (point < ROWS - HALO)
    upper = point >= ROWS - HALO
    base = jnp.where(
        inner, ((point - HALO) >> 8) * BLK, jnp.where(upper, ROWS - 2 * HALO, -HALO)
    )
    base = base + slab * ROWS
    low_bits = jnp.where(inner, BLK - 1, HALO - 1)
    lift = jnp.where(upper, HALO, 0)

    def tap_hits(t, carry):
        adj = adj_in[t]
        rel = adj - base
        near = jnp.where(adj < 0, -1, (rel & low_bits) + lift)
        sides[t] = rel
        hits[t] = onehot(iota((BLK, ROWS), 0) == near)
        return carry

    loads[2].wait()
    lax.fori_loop(0, 9, tap_hits, 0)
    for load in loads[3:]:
        load.wait()
    for i in range(3):
        lens[i * C : (i + 1) * C] = flip(lens_in[:, i * C : (i + 1) * C]).astype(BF16)
    mixer[...] = flip(mixer_in[...]).astype(BF16)
    for i in range(4):
        wide[i * C : (i + 1) * C] = flip(wide_in[:, i * C : (i + 1) * C]).astype(BF16)
        narrow[:, i * C : (i + 1) * C] = flip(narrow_in[i * C : (i + 1) * C]).astype(BF16)
    for t in range(TAPS):
        stencil[:, t * C : (t + 1) * C] = flip(stencil_in[t * C : (t + 1) * C]).astype(BF16)
    film = flip(jnp.concatenate([film_ref[...], jnp.zeros((6, C), F32)], axis=0))

    arrived(1)
    start(data_copies[3])
    arrived(4)
    start(meta_copies[1])
    mland[0] = mmid[0:8, 0]
    land[8] = mid[8:16, 0]
    lax.fori_loop(9, 15, tap_hits, 0)
    arrived(0)
    start(data_copies[2])
    land[0] = mid[0:8, 0]
    lax.fori_loop(15, TAPS, tap_hits, 0)
    arrived(5)
    places = jnp.concatenate([jnp.sum(mland[0:8], axis=1), jnp.sum(mland[8:16], axis=0)], axis=0)
    places = flip(places)
    for m in range(16):
        wants[m * C : (m + 1) * C] = onehot(
            (iota((C, ROWS), 1) + 1).astype(F32) == places[:, m : m + 1]
        )

    def unpack(m0):
        rows = [flip(land[m].reshape(C, C)).astype(BF16) for m in range(m0, m0 + 8)]
        return dot(jnp.concatenate(rows, axis=1), wants[m0 * C : (m0 + 8) * C])

    arrived(2)
    own = unpack(0)
    arrived(3)
    ext[:, HALO : HALO + ROWS] = (own + unpack(8)).astype(BF16)
    down = pltpu.make_async_remote_copy(
        ext.at[:, HALO : 2 * HALO], ext.at[:, EXT - HALO : EXT], hsem.at[0], hsem.at[1],
        device_id=slab_peer(-1), device_id_type=MESH,
    )
    up = pltpu.make_async_remote_copy(
        ext.at[:, ROWS : ROWS + HALO], ext.at[:, 0:HALO], hsem.at[2], hsem.at[3],
        device_id=slab_peer(1), device_id_type=MESH,
    )
    pl.when(slab > 0)(down.start)
    pl.when(slab < 127)(up.start)

    for b in range(3):
        at = HALO + b * BLK
        cols = slice(at, at + BLK)
        pair = jnp.concatenate([ext[:, at : at + BLK], ext[:, at + BLK : at + 2 * BLK]], axis=0)
        for t in range(TAPS):
            both = dot(pair, hits[t, :, cols])
            gathered[t * C : (t + 1) * C, cols] = jnp.where(
                sides[t, :, cols] >= BLK, both[C:], both[:C]
            ).astype(BF16)
        conv[:, cols] = dot(stencil[...], gathered[:, cols])

    @pl.when(slab > 0)
    def _():
        up.wait_recv()

    @pl.when(slab == 0)
    def _():
        ext[:, 0:HALO] = jnp.zeros((C, HALO), BF16)

    @pl.when(slab < 127)
    def _():
        down.wait_recv()

    @pl.when(slab == 127)
    def _():
        ext[:, EXT - HALO : EXT] = jnp.zeros((C, HALO), BF16)

    tail = ROWS - HALO
    trio = jnp.concatenate(
        [
            jnp.concatenate(
                [ext[:, w * HALO : (w + 1) * HALO], ext[:, tail + w * HALO : tail + (w + 1) * HALO]],
                axis=1,
            )
            for w in range(3)
        ],
        axis=0,
    )
    for t in range(TAPS):
        three = dot(trio, jnp.concatenate([hits[t, :, :HALO], hits[t, :, tail:]], axis=1))
        side = jnp.concatenate([sides[t, :, :HALO], sides[t, :, tail:]], axis=1)
        picked = jnp.where(
            side >= HALO, jnp.where(side >= 2 * HALO, three[2 * C :], three[C : 2 * C]), three[:C]
        ).astype(BF16)
        gathered[t * C : (t + 1) * C, :HALO] = picked[:, :HALO]
        gathered[t * C : (t + 1) * C, tail:] = picked[:, HALO:]
    ends = dot(stencil[...], jnp.concatenate([gathered[:, :HALO], gathered[:, tail:]], axis=1))
    conv[:, :HALO] = ends[:, :HALO]
    conv[:, tail:] = ends[:, HALO:]

    after_conv = ext[:, HALO : HALO + ROWS].astype(F32) + normalize(conv[...])
    conv[...] = after_conv
    normed = normalize(after_conv).astype(BF16)
    projected = dot(lens[...], normed)

    def unit(values):
        shaped = values.reshape(HEADS, C // HEADS, ROWS)
        power = jnp.mean(shaped * shaped, axis=1, keepdims=True)
        return (shaped * lax.rsqrt(jnp.maximum(power, 0.25))).reshape(C, ROWS)

    queries = unit(projected[:C]).astype(BF16)
    keys[...] = flip(unit(projected[C : 2 * C])).astype(BF16)
    values = projected[2 * C :].astype(BF16)
    ones = jnp.ones((C // HEADS, ROWS), BF16)
    head_of = iota((C, ROWS), 0) >> 4
    outs = [[] for _ in range(HEADS)]
    waiting = []

    def combine():
        h, weights = waiting.pop(0)
        value = jnp.concatenate([values[16 * h : 16 * h + 16], ones], axis=0)
        sums = dot(value, weights)
        outs[h].append(sums[:16] / sums[16:])

    for h in range(HEADS):
        query = jnp.where(head_of == h, queries, jnp.zeros_like(queries))
        for b in range(ROWS // BLK):
            scores = dot(keys[...], query[:, b * BLK : (b + 1) * BLK])
            waiting.append((h, jnp.exp2(scores * (sharp_ref[0, h] * (LOG2E / 16))).astype(BF16)))
            if len(waiting) > 1:
                combine()
    combine()
    mixed = jnp.concatenate([jnp.concatenate(parts, axis=1) for parts in outs], axis=0).astype(BF16)
    after_attn = conv[...] + dot(mixer[...], mixed)
    film_input = (normalize(after_attn) * (1.0 + film[:, 0:1]) + film[:, 1:2]).astype(BF16)
    hidden = jax.nn.gelu(dot(wide[...], film_input), approximate=True).astype(BF16)
    out_ref[...] = flip(after_attn + dot(narrow[...], hidden)).astype(BF16)
    for stage in range(6):
        pltpu.make_async_copy(landed[stage], landed[stage], ssem.at[stage]).wait()
    pl.when(slab > 0)(down.wait_send)
    pl.when(slab < 127)(up.wait_send)


def normalize(values):
    average = jnp.mean(values, axis=0, keepdims=True)
    centred = values - average
    spread = jnp.mean(centred * centred, axis=0, keepdims=True)
    return centred * lax.rsqrt(spread + 1e-05)


def shards(features, targets, adjacency, stencil, lens, sharp, mixer, film, wide, narrow):
    hbm = pl.BlockSpec(memory_space=pl.ANY)
    vmem = pl.BlockSpec(memory_space=pltpu.VMEM)
    smem = pl.BlockSpec(memory_space=pltpu.SMEM)
    hid = wide.shape[-1]
    return pl.pallas_call(
        block_kernel,
        out_shape=jax.ShapeDtypeStruct((ROWS, C), BF16),
        in_specs=[hbm] * 5 + [smem, hbm, vmem, hbm, hbm],
        out_specs=vmem,
        scratch_shapes=[
            pltpu.VMEM((ROWS, C), BF16),
            pltpu.VMEM((1, ROWS), I32),
            pltpu.VMEM((TAPS, 1, ROWS), I32),
            pltpu.VMEM((TAPS * C, C), BF16),
            pltpu.VMEM((C, 3 * C), BF16),
            pltpu.VMEM((C, C), BF16),
            pltpu.VMEM((C, hid), BF16),
            pltpu.VMEM((hid, C), BF16),
        ]
        + [pltpu.VMEM((16, 8, 16, C), BF16)] * 3
        + [pltpu.VMEM((8, 16, 128), F32)] * 2
        + [
            pltpu.VMEM((16, 8, 128), F32),
            pltpu.VMEM((2 * ROWS, ROWS), BF16),
            pltpu.VMEM((TAPS, BLK, ROWS), BF16),
            pltpu.VMEM((TAPS, 1, ROWS), I32),
            pltpu.VMEM((C, EXT), BF16),
            pltpu.VMEM((TAPS * C, ROWS), BF16),
            pltpu.VMEM((C, ROWS), F32),
            pltpu.VMEM((C, TAPS * C), BF16),
            pltpu.VMEM((3 * C, C), BF16),
            pltpu.VMEM((C, C), BF16),
            pltpu.VMEM((hid, C), BF16),
            pltpu.VMEM((C, hid), BF16),
            pltpu.VMEM((ROWS, C), BF16),
            pltpu.SemaphoreType.DMA((6,)),
            pltpu.SemaphoreType.DMA((6,)),
            pltpu.SemaphoreType.DMA((4,)),
            pltpu.SemaphoreType.DMA((8,)),
        ],
        compiler_params=pltpu.CompilerParams(
            collective_id=0, has_side_effects=True, vmem_limit_bytes=56 << 20
        ),
    )(
        features, targets, adjacency.reshape(TAPS, 1, ROWS), stencil.reshape(TAPS * C, C),
        lens[0], sharp, mixer[0], film.reshape(2, C), wide[0], narrow[0],
    )


def solution(mesh):
    rows = P(("tile", "pts", "grp"), None)
    in_specs = (
        rows,
        P(None, ("tile", "pts", "grp")),
        P(None, None, ("tile", "pts", "grp")),
        P(), P(), P(), P(), P("tile"), P(), P(),
    )
    return jax.shard_map(shards, mesh=mesh, in_specs=in_specs, out_specs=rows, check_vma=False)
```

```python
import functools

import jax
import jax.numpy as jnp
from jax import lax
from jax.experimental import pallas as pl
from jax.experimental.pallas import tpu as pltpu
from jax.sharding import PartitionSpec as P

MESH = pl.DeviceIdType.MESH
F32, BF16, I32 = jnp.float32, jnp.bfloat16, jnp.int32
ROWS = 1024
C = 128
HALO = 128
HEADS = 8
TAPS = 27
EXT = ROWS + 2 * HALO
BLK = 256
LOG2E = 1.4426950408889634


def dot(a, b):
    return jnp.dot(a, b, preferred_element_type=F32)


def dot_nt(a, b):
    return lax.dot_general(a, b, (((1,), (1,)), ((), ())), preferred_element_type=F32)


def onehot(mask):
    return jnp.where(mask, 1.0, 0.0).astype(BF16)


def flip(values):
    return jnp.transpose(values.astype(F32), (1, 0))


def iota(shape, dim):
    return lax.broadcasted_iota(I32, shape, dim)


def z_peer(dz):
    return (lax.axis_index("tile"), lax.axis_index("pts"), (lax.axis_index("grp") + dz) & 7)


def xy_peer(half, idx):
    me = lax.axis_index("pts")
    dy = idx >> 1
    dx = 2 * (idx & 1) + ((half + dy) & 1)
    return (
        lax.axis_index("tile"),
        (((me >> 2) + dy) & 3) * 4 + (((me & 3) + dx) & 3),
        lax.axis_index("grp"),
    )


def slab_peer(step):
    me = (lax.axis_index("pts") * 8 + lax.axis_index("grp") + step) & 127
    return (lax.axis_index("tile"), me >> 3, me & 7)


def block_kernel(
    x_hbm, target_hbm, adj_hbm, stencil_hbm, lens_hbm, sharp_ref, mixer_hbm, film_ref, wide_hbm,
    narrow_hbm, out_ref, x, target_in, adj_in, stencil_in, lens_in, mixer_in, wide_in, narrow_in,
    send, mid, land, msend, mmid, mland, wants, hits, sides, ext, gathered, conv,
    stencil, lens, mixer, wide, narrow, keys, ssem, rsem, hsem, isem,
):
    pts, grp = lax.axis_index("pts"), lax.axis_index("grp")
    loads = [
        pltpu.make_async_copy(src, dst, isem.at[i])
        for i, (src, dst) in enumerate(
            (
                (target_hbm, target_in), (x_hbm, x), (adj_hbm, adj_in), (lens_hbm, lens_in),
                (mixer_hbm, mixer_in), (wide_hbm, wide_in), (narrow_hbm, narrow_in),
                (stencil_hbm, stencil_in),
            )
        )
    ]
    loads[0].start()
    loads[1].start()
    peers = [z_peer(i) for i in range(1, 8)]
    peers += [xy_peer(0, i) for i in range(1, 8)] + [xy_peer(1, i) for i in range(8)]
    slab = pts * 8 + grp
    barrier = pltpu.get_barrier_semaphore()

    def greet(peer):
        pl.semaphore_signal(barrier, inc=1, device_id=peer, device_id_type=MESH)

    for peer in peers:
        greet(peer)
    pl.when(slab > 0)(lambda: greet(slab_peer(-1)))
    pl.when(slab < 127)(lambda: greet(slab_peer(1)))
    for load in loads[2:]:
        load.start()

    loads[0].wait()
    target = target_in[...]
    owner = target >> 10
    dy = ((owner >> 5) - (pts >> 2)) & 3
    dx = ((owner >> 3) - (pts & 3)) & 3
    dz = (owner - grp) & 7
    flat = dy * 2 + (dx >> 1)
    odd = (dx + dy) & 1
    group = jnp.where(odd == 0, dz * 8 + flat, 64 + flat * 8 + dz)
    member = iota((128, ROWS), 0) == group
    member_bf = onehot(member)
    earlier = onehot(iota((BLK, BLK), 0) < iota((BLK, BLK), 1))
    carry = jnp.zeros((128, 1), F32)
    ranks = []
    for b in range(ROWS // BLK):
        cols = slice(b * BLK, (b + 1) * BLK)
        part = member_bf[:, cols]
        count = dot(part, earlier) + carry
        ranks.append(jnp.sum(jnp.where(member[:, cols], count, 0.0), axis=0, keepdims=True))
        if b < ROWS // BLK - 1:
            carry = carry + jnp.sum(part.astype(F32), axis=1, keepdims=True)
    rank = jnp.concatenate(ranks, axis=1).astype(I32)
    slot = group * 16 + rank
    loads[1].wait()

    def pack(m0):
        hit = onehot(iota((512, ROWS), 0) + m0 * 128 == slot)
        return dot(hit, x[...]).astype(BF16).reshape(4, 8, 16, C)

    packed = pack(0)
    send[0:4] = packed
    mid[0] = packed[0]

    inward = jnp.minimum(slab, 1) + jnp.minimum(127 - slab, 1)
    pl.semaphore_wait(barrier, len(peers) + inward)

    def remote(stage, src, dst, peer):
        return pltpu.make_async_remote_copy(
            src, dst, ssem.at[stage], rsem.at[stage], device_id=peer, device_id_type=MESH
        )

    data_copies = (
        [remote(0, send.at[i], mid.at[i], z_peer(i)) for i in range(1, 8)],
        [remote(1, send.at[8 + i], mid.at[8 + i], xy_peer(1, i)) for i in range(8)],
        [remote(2, mid.at[0:8, i], land.at[i], xy_peer(0, i)) for i in range(1, 8)],
        [remote(3, mid.at[8:16, i], land.at[8 + i], z_peer(i)) for i in range(1, 8)],
    )
    meta_copies = (
        [remote(4, msend.at[i], mmid.at[i], z_peer(i)) for i in range(1, 8)],
        [
            remote(5, mmid.at[0:8, i], mland.at[i], xy_peer(i >> 3, i & 7)) for i in range(1, 16)
        ],
    )
    landed = (
        mid.at[1:8], mid.at[8:16], land.at[1:8], land.at[9:16], mmid.at[1:8], mland.at[1:16]
    )

    def start(copies):
        for copy in copies:
            copy.start()

    def arrived(stage):
        pltpu.make_async_copy(landed[stage], landed[stage], rsem.at[stage]).wait()

    start(data_copies[0][0:3])
    send[4:8] = pack(4)
    start(data_copies[0][3:7])
    for m0 in (8, 12):
        send[m0 : m0 + 4] = pack(m0)
        start(data_copies[1][m0 - 8 : m0 - 4])
    lane = ((group >> 3) & 7) * 16 + rank
    place = (target & 1023) + 1
    here = iota((128, ROWS), 0) == lane
    high = jnp.where(here, (place >> 5).astype(F32), 0.0).astype(BF16)
    low = jnp.where(here, (place & 31).astype(F32), 0.0).astype(BF16)
    by_z = onehot(iota((128, ROWS), 0) == dz * 16 + odd * 8 + flat)
    meta = (32.0 * dot_nt(by_z, high) + dot_nt(by_z, low)).reshape(8, 16, 128)
    msend[...] = meta
    mmid[0] = meta[0]
    start(meta_copies[0])

    point = iota((1, ROWS), 1)
    inner = (point >= HALO) & (point < ROWS - HALO)
    upper = point >= ROWS - HALO
    base = jnp.where(
        inner, ((point - HALO) >> 8) * BLK, jnp.where(upper, ROWS - 2 * HALO, -HALO)
    )
    base = base + slab * ROWS
    low_bits = jnp.where(inner, BLK - 1, HALO - 1)
    lift = jnp.where(upper, HALO, 0)

    def tap_hits(t, carry):
        adj = adj_in[t]
        rel = adj - base
        near = jnp.where(adj < 0, -1, (rel & low_bits) + lift)
        sides[t] = rel
        hits[t] = onehot(iota((BLK, ROWS), 0) == near)
        return carry

    loads[2].wait()
    lax.fori_loop(0, 9, tap_hits, 0)
    for load in loads[3:]:
        load.wait()
    for i in range(3):
        lens[i * C : (i + 1) * C] = flip(lens_in[:, i * C : (i + 1) * C]).astype(BF16)
    mixer[...] = flip(mixer_in[...]).astype(BF16)
    for i in range(4):
        wide[i * C : (i + 1) * C] = flip(wide_in[:, i * C : (i + 1) * C]).astype(BF16)
        narrow[:, i * C : (i + 1) * C] = flip(narrow_in[i * C : (i + 1) * C]).astype(BF16)
    for t in range(TAPS):
        stencil[:, t * C : (t + 1) * C] = flip(stencil_in[t * C : (t + 1) * C]).astype(BF16)
    film = flip(jnp.concatenate([film_ref[...], jnp.zeros((6, C), F32)], axis=0))

    arrived(1)
    start(data_copies[3])
    arrived(4)
    start(meta_copies[1])
    mland[0] = mmid[0:8, 0]
    land[8] = mid[8:16, 0]
    lax.fori_loop(9, 15, tap_hits, 0)
    arrived(0)
    start(data_copies[2])
    land[0] = mid[0:8, 0]
    lax.fori_loop(15, TAPS, tap_hits, 0)
    arrived(5)
    places = jnp.concatenate([jnp.sum(mland[0:8], axis=1), jnp.sum(mland[8:16], axis=0)], axis=0)
    places = flip(places)
    for m in range(16):
        wants[m * C : (m + 1) * C] = onehot(
            (iota((C, ROWS), 1) + 1).astype(F32) == places[:, m : m + 1]
        )

    tail = ROWS - HALO

    def turned(m0):
        rows = [flip(land[m].reshape(C, C)).astype(BF16) for m in range(m0, m0 + 8)]
        return jnp.concatenate(rows, axis=1)

    def unpack(rows, m0):
        half = wants[m0 * C : (m0 + 8) * C]
        rim = jnp.concatenate([half[:, :HALO], half[:, tail:]], axis=1)
        return dot(rows, rim), dot(rows, half[:, HALO:tail])

    arrived(2)
    rim, inside = unpack(turned(0), 0)
    arrived(3)
    more_rim, more_inside = unpack(turned(8), 8)
    rim = (rim + more_rim).astype(BF16)
    ext[:, HALO : 2 * HALO] = rim[:, :HALO]
    ext[:, ROWS : ROWS + HALO] = rim[:, HALO:]
    down = pltpu.make_async_remote_copy(
        ext.at[:, HALO : 2 * HALO], ext.at[:, EXT - HALO : EXT], hsem.at[0], hsem.at[1],
        device_id=slab_peer(-1), device_id_type=MESH,
    )
    up = pltpu.make_async_remote_copy(
        ext.at[:, ROWS : ROWS + HALO], ext.at[:, 0:HALO], hsem.at[2], hsem.at[3],
        device_id=slab_peer(1), device_id_type=MESH,
    )
    pl.when(slab > 0)(down.start)
    pl.when(slab < 127)(up.start)
    ext[:, 2 * HALO : ROWS] = (inside + more_inside).astype(BF16)

    for b in range(3):
        at = HALO + b * BLK
        cols = slice(at, at + BLK)
        pair = jnp.concatenate([ext[:, at : at + BLK], ext[:, at + BLK : at + 2 * BLK]], axis=0)
        for t in range(TAPS):
            both = dot(pair, hits[t, :, cols])
            gathered[t * C : (t + 1) * C, cols] = jnp.where(
                sides[t, :, cols] >= BLK, both[C:], both[:C]
            ).astype(BF16)
        conv[:, cols] = dot(stencil[...], gathered[:, cols])

    @pl.when(slab > 0)
    def _():
        up.wait_recv()

    @pl.when(slab == 0)
    def _():
        ext[:, 0:HALO] = jnp.zeros((C, HALO), BF16)

    @pl.when(slab < 127)
    def _():
        down.wait_recv()

    @pl.when(slab == 127)
    def _():
        ext[:, EXT - HALO : EXT] = jnp.zeros((C, HALO), BF16)

    trio = jnp.concatenate(
        [
            jnp.concatenate(
                [ext[:, w * HALO : (w + 1) * HALO], ext[:, tail + w * HALO : tail + (w + 1) * HALO]],
                axis=1,
            )
            for w in range(3)
        ],
        axis=0,
    )
    for t in range(TAPS):
        three = dot(trio, jnp.concatenate([hits[t, :, :HALO], hits[t, :, tail:]], axis=1))
        side = jnp.concatenate([sides[t, :, :HALO], sides[t, :, tail:]], axis=1)
        picked = jnp.where(
            side >= HALO, jnp.where(side >= 2 * HALO, three[2 * C :], three[C : 2 * C]), three[:C]
        ).astype(BF16)
        gathered[t * C : (t + 1) * C, :HALO] = picked[:, :HALO]
        gathered[t * C : (t + 1) * C, tail:] = picked[:, HALO:]
    ends = dot(stencil[...], jnp.concatenate([gathered[:, :HALO], gathered[:, tail:]], axis=1))
    conv[:, :HALO] = ends[:, :HALO]
    conv[:, tail:] = ends[:, HALO:]

    after_conv = ext[:, HALO : HALO + ROWS].astype(F32) + normalize(conv[...])
    conv[...] = after_conv
    normed = normalize(after_conv).astype(BF16)
    projected = dot(lens[...], normed)

    def unit(values):
        shaped = values.reshape(HEADS, C // HEADS, ROWS)
        power = jnp.mean(shaped * shaped, axis=1, keepdims=True)
        return (shaped * lax.rsqrt(jnp.maximum(power, 0.25))).reshape(C, ROWS)

    queries = unit(projected[:C]).astype(BF16)
    keys[...] = flip(unit(projected[C : 2 * C])).astype(BF16)
    values = projected[2 * C :].astype(BF16)
    ones = jnp.ones((C // HEADS, ROWS), BF16)
    head_of = iota((C, ROWS), 0) >> 4
    outs = [[] for _ in range(HEADS)]
    waiting = []

    def combine():
        h, weights = waiting.pop(0)
        value = jnp.concatenate([values[16 * h : 16 * h + 16], ones], axis=0)
        sums = dot(value, weights)
        outs[h].append(sums[:16] / sums[16:])

    for h in range(HEADS):
        query = jnp.where(head_of == h, queries, jnp.zeros_like(queries))
        for b in range(ROWS // BLK):
            scores = dot(keys[...], query[:, b * BLK : (b + 1) * BLK])
            waiting.append((h, jnp.exp2(scores * (sharp_ref[0, h] * (LOG2E / 16))).astype(BF16)))
            if len(waiting) > 1:
                combine()
    combine()
    mixed = jnp.concatenate([jnp.concatenate(parts, axis=1) for parts in outs], axis=0).astype(BF16)
    after_attn = conv[...] + dot(mixer[...], mixed)
    film_input = (normalize(after_attn) * (1.0 + film[:, 0:1]) + film[:, 1:2]).astype(BF16)
    hidden = jax.nn.gelu(dot(wide[...], film_input), approximate=True).astype(BF16)
    out_ref[...] = flip(after_attn + dot(narrow[...], hidden)).astype(BF16)
    for stage in range(6):
        pltpu.make_async_copy(landed[stage], landed[stage], ssem.at[stage]).wait()
    pl.when(slab > 0)(down.wait_send)
    pl.when(slab < 127)(up.wait_send)


def normalize(values):
    average = jnp.mean(values, axis=0, keepdims=True)
    centred = values - average
    spread = jnp.mean(centred * centred, axis=0, keepdims=True)
    return centred * lax.rsqrt(spread + 1e-05)


def shards(features, targets, adjacency, stencil, lens, sharp, mixer, film, wide, narrow):
    hbm = pl.BlockSpec(memory_space=pl.ANY)
    vmem = pl.BlockSpec(memory_space=pltpu.VMEM)
    smem = pl.BlockSpec(memory_space=pltpu.SMEM)
    hid = wide.shape[-1]
    return pl.pallas_call(
        block_kernel,
        out_shape=jax.ShapeDtypeStruct((ROWS, C), BF16),
        in_specs=[hbm] * 5 + [smem, hbm, vmem, hbm, hbm],
        out_specs=vmem,
        scratch_shapes=[
            pltpu.VMEM((ROWS, C), BF16),
            pltpu.VMEM((1, ROWS), I32),
            pltpu.VMEM((TAPS, 1, ROWS), I32),
            pltpu.VMEM((TAPS * C, C), BF16),
            pltpu.VMEM((C, 3 * C), BF16),
            pltpu.VMEM((C, C), BF16),
            pltpu.VMEM((C, hid), BF16),
            pltpu.VMEM((hid, C), BF16),
        ]
        + [pltpu.VMEM((16, 8, 16, C), BF16)] * 3
        + [pltpu.VMEM((8, 16, 128), F32)] * 2
        + [
            pltpu.VMEM((16, 8, 128), F32),
            pltpu.VMEM((2 * ROWS, ROWS), BF16),
            pltpu.VMEM((TAPS, BLK, ROWS), BF16),
            pltpu.VMEM((TAPS, 1, ROWS), I32),
            pltpu.VMEM((C, EXT), BF16),
            pltpu.VMEM((TAPS * C, ROWS), BF16),
            pltpu.VMEM((C, ROWS), F32),
            pltpu.VMEM((C, TAPS * C), BF16),
            pltpu.VMEM((3 * C, C), BF16),
            pltpu.VMEM((C, C), BF16),
            pltpu.VMEM((hid, C), BF16),
            pltpu.VMEM((C, hid), BF16),
            pltpu.VMEM((ROWS, C), BF16),
            pltpu.SemaphoreType.DMA((6,)),
            pltpu.SemaphoreType.DMA((6,)),
            pltpu.SemaphoreType.DMA((4,)),
            pltpu.SemaphoreType.DMA((8,)),
        ],
        compiler_params=pltpu.CompilerParams(
            collective_id=0, has_side_effects=True, vmem_limit_bytes=56 << 20
        ),
    )(
        features, targets, adjacency.reshape(TAPS, 1, ROWS), stencil.reshape(TAPS * C, C),
        lens[0], sharp, mixer[0], film.reshape(2, C), wide[0], narrow[0],
    )


def solution(mesh):
    rows = P(("tile", "pts", "grp"), None)
    in_specs = (
        rows,
        P(None, ("tile", "pts", "grp")),
        P(None, None, ("tile", "pts", "grp")),
        P(), P(), P(), P(), P("tile"), P(), P(),
    )
    return jax.shard_map(shards, mesh=mesh, in_specs=in_specs, out_specs=rows, check_vma=False)
```
